32 devices in a mesh: fsdp: 2 (over y), context: 4 (over z), tensor: 4 (over x, core).
Axes of the slice: x: 2, y: 2, z: 4, core: 2. Of those that a mesh axis runs over, the one named last changes fastest.
Arguments:
- tokens: bfloat16 [2, 1088, 1024], P('fsdp', 'context'), may hold values from -6 to 6
- segments: int32 [2, 1088], P('fsdp', 'context'), may hold values from 0 to 3, as said below
- cotangent: bfloat16 [2, 1088, 1024], P('fsdp', 'context'), may hold values from -6 to 6
- w_qkv: bfloat16 [1024, 3, 1024], P('fsdp', None, 'tensor'), may hold values from -0.1875 to 0.1875
- b_qv: bfloat16 [2, 16, 64], P(None, 'tensor', 'fsdp'), may hold values from -1.5 to 1.5
- w_out: bfloat16 [1024, 1024], P('tensor', 'fsdp'), may hold values from -1.5 to 1.5
- b_out: bfloat16 [1024], P('fsdp'), may hold values from -1.5 to 1.5
- w_fc: bfloat16 [1024, 4096], P('fsdp', 'tensor'), may hold values from -0.1875 to 0.1875
- b_fc: bfloat16 [16, 256], P('tensor', 'fsdp'), may hold values from -1.5 to 1.5
- w_proj: bfloat16 [4096, 1024], P('tensor', 'fsdp'), may hold values from -0.09375 to 0.09375
- b_proj: bfloat16 [1024], P('fsdp'), may hold values from -1.5 to 1.5
- ln1_gain: bfloat16 [1024], P('fsdp'), may hold values from 0.25 to 1.75
- ln1_shift: bfloat16 [1024], P('fsdp'), may hold values from -1.5 to 1.5
- ln2_gain: bfloat16 [1024], P('fsdp'), may hold values from 0.25 to 1.75
- ln2_shift: bfloat16 [1024], P('fsdp'), may hold values from -1.5 to 1.5
Outputs:
- mixed: bfloat16 [2, 1088, 1024], P('fsdp', 'context')
- grad_tokens: float32 [2, 1088, 1024], P('fsdp', 'context')
- grad_w_qkv: float32 [1024, 3, 1024], P('fsdp', None, 'tensor')
- grad_b_qv: float32 [2, 16, 64], P(None, 'tensor', 'fsdp')
- grad_w_out: float32 [1024, 1024], P('tensor', 'fsdp')
- grad_b_out: float32 [1024], P('fsdp')
- grad_w_fc: float32 [1024, 4096], P('fsdp', 'tensor')
- grad_b_fc: float32 [16, 256], P('tensor', 'fsdp')
- grad_w_proj: float32 [4096, 1024], P('tensor', 'fsdp')
- grad_b_proj: float32 [1024], P('fsdp')
- grad_ln1_gain: float32 [1024], P('fsdp')
- grad_ln1_shift: float32 [1024], P('fsdp')
- grad_ln2_gain: float32 [1024], P('fsdp')
- grad_ln2_shift: float32 [1024], P('fsdp')
The draws below stay inside these ranges and needn't reach their ends.
Inputs may be any that keep to these rules, and one draw needn't show every extreme that they name: `segments`: in each of the 2 rows the sequence numbers run 0, 1, 2, 3 in order, each present; sequence 1 has exactly 1024 positions and starts within the first 272 positions of its row.
All inputs are finite; a program needn't handle non-finite values.
Results may differ from the reference program's by a relative error of at most 0.017.
Values may be sent and summed in bfloat16 or wider, within the bound.
A program may use at most 128 MiB of HBM per device.

```python
import jax
import jax.numpy as jnp
from jax import lax

D = 1024
HEADS = 16
HD = 64
FF = 4096
SPAN = 1024
STRETCH = 272
GROUP_TOK = 1088
PACKS_ALL = 2


def draw_segments(key, part):
    key = jax.random.fold_in(key, 7)
    key_first, key_last = jax.random.split(key)
    first = jax.random.randint(key_first, (PACKS_ALL, 1), 1, min(STRETCH, GROUP_TOK - SPAN - 1))
    spare = GROUP_TOK - SPAN - 1 - first
    offset = jax.random.randint(key_last, (PACKS_ALL, 1), 0, 1 << 20) % spare
    last = first + SPAN + 1 + offset
    position = jnp.arange(GROUP_TOK, dtype=jnp.int32)[None, :]
    return (position >= first).astype(jnp.int32) + (position >= first + SPAN).astype(jnp.int32) + (position >= last).astype(jnp.int32)


def steps_of(stream_key, shape, shards, low, top_value):
    loudness = 1.0
    for axis_at, parts in shards:
        steps = jax.random.uniform(jax.random.fold_in(jax.random.fold_in(stream_key, 6), axis_at), (parts,), jnp.float32, low / len(shards), top_value / len(shards))
        loudness = loudness * jnp.repeat(jnp.exp(steps), shape[axis_at] // parts).reshape((-1,) + (1,) * (len(shape) - 1 - axis_at))
    return loudness


def gaussian(key, extent, deviation, reach, pieces=(), kind=jnp.bfloat16):
    level = steps_of(key, extent, pieces, -0.22, 0.18) if pieces else 1.0
    result = jax.random.normal(key, extent, jnp.float32) * deviation * level
    return jnp.minimum(jnp.maximum(result, -reach), reach).astype(kind)


def setup_inputs(seed: int = 0) -> dict:
    splits = jax.random.split(jax.random.key(seed), 16)
    return {
        "tokens": gaussian(splits[0], (PACKS_ALL, GROUP_TOK, D), 1.0, 6.0, ((0, 2), (1, 4))),
        "segments": draw_segments(jax.random.fold_in(splits[15], 71), 0),
        "cotangent": gaussian(splits[2], (PACKS_ALL, GROUP_TOK, D), 1.0, 6.0, ((0, 2), (1, 4))),
        "w_qkv": gaussian(splits[3], (D, 3, D), D ** -0.5, 0.1875, ((0, 2), (2, 4))),
        "b_qv": gaussian(splits[4], (2, HEADS, HD), 0.3, 1.5, ((1, 4), (2, 2))),
        "w_out": gaussian(splits[5], (D, D), (D // 64) ** -0.5, 1.5, ((0, 4), (1, 2))),
        "b_out": gaussian(splits[6], (D,), 0.3, 1.5, ((0, 2),)),
        "w_fc": gaussian(splits[7], (D, FF), D ** -0.5, 0.1875, ((0, 2), (1, 4))),
        "b_fc": gaussian(splits[8], (HEADS, FF // HEADS), 0.3, 1.5, ((0, 4), (1, 2))),
        "w_proj": gaussian(splits[9], (FF, D), FF ** -0.5, 0.09375, ((0, 4), (1, 2))),
        "b_proj": gaussian(splits[10], (D,), 0.3, 1.5, ((0, 2),)),
        "ln1_gain": jnp.clip(1.0 + 0.15 * jax.random.normal(splits[11], (D,), jnp.float32), 0.25, 1.75).astype(jnp.bfloat16),
        "ln1_shift": gaussian(splits[12], (D,), 0.3, 1.5, ((0, 2),)),
        "ln2_gain": jnp.clip(1.0 + 0.15 * jax.random.normal(splits[13], (D,), jnp.float32), 0.25, 1.75).astype(jnp.bfloat16),
        "ln2_shift": gaussian(splits[14], (D,), 0.3, 1.5, ((0, 2),)),
    }


@jax.custom_vjp
def low(v):
    return lax.optimization_barrier(v.astype(jnp.bfloat16)).astype(jnp.float32)

@jax.custom_vjp
def low_back(v):
    return v

def low_keep(v):
    return (low(v), None)

def low_pass(kept, grad):
    return (grad,)

def back_keep(v):
    return (v, None)

def back_low(kept, grad):
    return (low(grad),)
low.defvjp(low_keep, low_pass)
low_back.defvjp(back_keep, back_low)
EPSILON = 1e-05
MASK_FILL = 1e+30
SCORE_SCALE = 0.125
PRECISE = lax.Precision.HIGHEST

def layer_norm(values, gain, shift):
    mean = lax.optimization_barrier(jnp.mean(values, axis=-1, keepdims=True))
    centred = values - mean
    spread = lax.optimization_barrier(jnp.mean(centred * centred, axis=-1, keepdims=True))
    return centred * lax.rsqrt(spread + EPSILON) * gain + shift

def gelu_tanh(values):
    inner = 0.7978845608028654 * (values + 0.044715 * values * values * values)
    return 0.5 * values * (1.0 + jnp.tanh(inner))

def attend_pack(inputs):
    queries, keys, values, segments = inputs
    length = segments.shape[0]
    query_heads = queries.reshape(length, HEADS, HD)
    key_heads = keys.reshape(length, HEADS, HD)
    value_heads = values.reshape(length, HEADS, HD)
    raw_scores = jnp.einsum('qhe,khe->hqk', query_heads, key_heads, precision=PRECISE)
    scores = low_back(SCORE_SCALE * raw_scores)
    position = jnp.arange(length, dtype=jnp.int32)
    seen = (segments[:, None] == segments[None, :]) & (position[None, :] <= position[:, None])
    scores = jnp.where(seen[None], scores, -MASK_FILL)
    row_top = lax.optimization_barrier(jnp.max(scores, axis=-1, keepdims=True))
    exponent = jnp.exp(scores - row_top)
    probs = low(exponent / lax.optimization_barrier(jnp.sum(exponent, axis=-1, keepdims=True)))
    attended = jnp.einsum('hqk,khe->qhe', probs, value_heads, precision=PRECISE)
    return attended.reshape(length, HEADS * HD)

def forward(tokens, w_qkv, b_qv, w_out, b_out, w_fc, b_fc, w_proj, b_proj, ln1_gain, ln1_shift, ln2_gain, ln2_shift, segments):
    normed1 = low(layer_norm(tokens, ln1_gain, ln1_shift))
    bias_qv = b_qv.reshape(2, D)
    queries = low_back(low(jnp.einsum('ptd,de->pte', normed1, w_qkv[:, 0], precision=PRECISE) + bias_qv[0]))
    keys = low_back(low(jnp.einsum('ptd,de->pte', normed1, w_qkv[:, 1], precision=PRECISE)))
    values = low_back(low(jnp.einsum('ptd,de->pte', normed1, w_qkv[:, 2], precision=PRECISE) + bias_qv[1]))
    attended = lax.map(jax.checkpoint(attend_pack), (queries, keys, values, segments))
    attended = low_back(low(attended))
    hidden_state = tokens + low_back(jnp.einsum('pte,ed->ptd', attended, w_out, precision=PRECISE)) + b_out
    normed2 = low(layer_norm(hidden_state, ln2_gain, ln2_shift))
    pre_act = low_back(jnp.einsum('ptd,df->ptf', normed2, w_fc, precision=PRECISE) + b_fc.reshape(FF))
    activ = low(gelu_tanh(pre_act))
    return hidden_state + low_back(jnp.einsum('ptf,fd->ptd', activ, w_proj, precision=PRECISE)) + b_proj

def reference(tokens, segments, cotangent, w_qkv, b_qv, w_out, b_out, w_fc, b_fc, w_proj, b_proj, ln1_gain, ln1_shift, ln2_gain, ln2_shift):
    floats = (tokens.astype(jnp.float32), w_qkv.astype(jnp.float32), b_qv.astype(jnp.float32), w_out.astype(jnp.float32), b_out.astype(jnp.float32), w_fc.astype(jnp.float32), b_fc.astype(jnp.float32), w_proj.astype(jnp.float32), b_proj.astype(jnp.float32), ln1_gain.astype(jnp.float32), ln1_shift.astype(jnp.float32), ln2_gain.astype(jnp.float32), ln2_shift.astype(jnp.float32))

    def wrapped(*weights_in):
        return forward(*weights_in, segments)
    mixed, pullback = jax.vjp(wrapped, *floats)
    grads = pullback(cotangent.astype(jnp.float32))
    return (mixed.astype(jnp.bfloat16), grads[0], grads[1], grads[2], grads[3], grads[4], grads[5], grads[6], grads[7], grads[8], grads[9], grads[10], grads[11], grads[12])
```

```python
import jax
import jax.numpy as jnp
from jax import lax
from jax.sharding import PartitionSpec as P

HD = 64


EPSILON = 1e-05
MASK_FILL = 1e30
SCORE_SCALE = 0.125


def layer_norm(values, gain, shift):
    mean = jnp.mean(values, axis=-1, keepdims=True)
    centred = values - mean
    spread = jnp.mean(centred * centred, axis=-1, keepdims=True)
    return centred * lax.rsqrt(spread + EPSILON) * gain + shift


def gelu_tanh(values):
    inner = 0.7978845608028654 * (values + 0.044715 * values * values * values)
    return 0.5 * values * (1.0 + jnp.tanh(inner))


def visible(segments, key_segments, first_row):
    row_count = segments.shape[1]
    query_pos = first_row + jnp.arange(row_count, dtype=jnp.int32)
    key_pos = jnp.arange(key_segments.shape[1], dtype=jnp.int32)
    same = segments.astype(jnp.float32)[:, :, None] == key_segments.astype(jnp.float32)[:, None, :]
    return same & (key_pos[None, None, :] <= query_pos[None, :, None])


def scores_of(queries, keys_all, key_mask):
    raw_scores = jnp.einsum(
        "pqhe,pkhe->phqk", queries, keys_all, preferred_element_type=jnp.float32
    )
    return jnp.where(key_mask[:, None], SCORE_SCALE * raw_scores, -MASK_FILL)


def body(
    tokens,
    segments,
    cotangent,
    w_qkv,
    b_qv,
    w_out,
    b_out,
    w_fc,
    b_fc,
    w_proj,
    b_proj,
    ln1_gain,
    ln1_shift,
    ln2_gain,
    ln2_shift,
):
    pack_count, row_count, model_width = tokens.shape
    head_count = b_qv.shape[1]
    local_width = head_count * HD
    gathered = (
        lax.all_gather(w_qkv, "fsdp", axis=0, tiled=True),
        lax.all_gather(w_out, "fsdp", axis=1, tiled=True),
        lax.all_gather(w_fc, "fsdp", axis=0, tiled=True),
        lax.all_gather(w_proj, "fsdp", axis=1, tiled=True),
        lax.all_gather(b_qv, "fsdp", axis=2, tiled=True),
        lax.all_gather(b_out, "fsdp", axis=0, tiled=True),
        lax.all_gather(b_fc, "fsdp", axis=1, tiled=True),
        lax.all_gather(b_proj, "fsdp", axis=0, tiled=True),
        lax.all_gather(ln1_gain, "fsdp", axis=0, tiled=True),
        lax.all_gather(ln1_shift, "fsdp", axis=0, tiled=True),
        lax.all_gather(ln2_gain, "fsdp", axis=0, tiled=True),
        lax.all_gather(ln2_shift, "fsdp", axis=0, tiled=True),
    )
    qkv_all = gathered[0]
    out_all = gathered[1]
    fc_all = gathered[2]
    proj_all = gathered[3]
    bias_qv = gathered[4].astype(jnp.float32).reshape(2, local_width)
    bias_out = gathered[5].astype(jnp.float32)
    bias_fc = gathered[6].astype(jnp.float32).reshape(-1)
    bias_proj = gathered[7].astype(jnp.float32)
    gain_one = gathered[8].astype(jnp.float32)
    shift_one = gathered[9].astype(jnp.float32)
    gain_two = gathered[10].astype(jnp.float32)
    shift_two = gathered[11].astype(jnp.float32)
    first_row = lax.axis_index("context") * row_count
    base_rows = tokens.astype(jnp.float32)
    normed1 = layer_norm(base_rows, gain_one, shift_one).astype(jnp.bfloat16)
    projected = jnp.einsum("ptd,dje->ptje", normed1, qkv_all, preferred_element_type=jnp.float32)
    queries_low = (projected[:, :, 0] + bias_qv[0]).astype(jnp.bfloat16)
    keys_low = projected[:, :, 1].astype(jnp.bfloat16)
    values_low = (projected[:, :, 2] + bias_qv[1]).astype(jnp.bfloat16)
    seg_low = segments.astype(jnp.bfloat16)
    fetched = (
        lax.all_gather(keys_low, "context", axis=1, tiled=True),
        lax.all_gather(values_low, "context", axis=1, tiled=True),
        lax.all_gather(seg_low, "context", axis=1, tiled=True),
    )
    keys_all = fetched[0].reshape(pack_count, -1, head_count, HD)
    values_all = fetched[1].reshape(pack_count, -1, head_count, HD)
    key_mask = visible(segments, fetched[2], first_row)
    queries = queries_low.reshape(pack_count, row_count, head_count, HD)
    scores = scores_of(queries, keys_all, key_mask)
    row_top = jnp.max(scores, axis=-1, keepdims=True)
    exponent = jnp.exp(scores - row_top)
    row_total = jnp.sum(exponent, axis=-1, keepdims=True)
    probs = (exponent / row_total).astype(jnp.bfloat16)
    logsum = row_top + jnp.log(row_total)
    attended = jnp.einsum("phqk,pkhe->pqhe", probs, values_all, preferred_element_type=jnp.float32)
    attended = attended.reshape(pack_count, row_count, local_width).astype(jnp.bfloat16)
    attn_part = jnp.einsum("pte,ed->ptd", attended, out_all, preferred_element_type=jnp.float32)
    hidden_state = base_rows + lax.psum(attn_part, "tensor") + bias_out
    normed2 = layer_norm(hidden_state, gain_two, shift_two).astype(jnp.bfloat16)
    pre_act = (
        jnp.einsum("ptd,df->ptf", normed2, fc_all, preferred_element_type=jnp.float32) + bias_fc
    )
    activ = gelu_tanh(pre_act).astype(jnp.bfloat16)
    mlp_part = jnp.einsum("ptf,fd->ptd", activ, proj_all, preferred_element_type=jnp.float32)
    mixed = (
        hidden_state
        + lax.psum(mlp_part.astype(jnp.bfloat16), "tensor").astype(jnp.float32)
        + bias_proj
    ).astype(jnp.bfloat16)
    grad_out = cotangent.astype(jnp.float32)
    grad_b_proj = jnp.sum(grad_out, axis=(0, 1))
    grad_w_proj = jnp.einsum("ptf,ptd->fd", activ, cotangent, preferred_element_type=jnp.float32)
    grad_activ = jnp.einsum("ptd,fd->ptf", cotangent, proj_all, preferred_element_type=jnp.float32)
    unused, gelu_pull = jax.vjp(gelu_tanh, pre_act)
    grad_pre = gelu_pull(grad_activ)[0].astype(jnp.bfloat16)
    grad_b_fc = jnp.sum(grad_pre.astype(jnp.float32), axis=(0, 1)).reshape(gathered[6].shape)
    grad_w_fc = jnp.einsum("ptd,ptf->df", normed2, grad_pre, preferred_element_type=jnp.float32)
    grad_normed2 = jnp.einsum("ptf,df->ptd", grad_pre, fc_all, preferred_element_type=jnp.float32)
    grad_normed2 = lax.psum(grad_normed2, "tensor")
    unused_two, norm_pull = jax.vjp(layer_norm, hidden_state, gain_two, shift_two)
    grad_hidden_norm, grad_gain_two, grad_shift_two = norm_pull(grad_normed2)
    grad_hidden = grad_out + grad_hidden_norm
    grad_branch = grad_hidden.astype(jnp.bfloat16)
    grad_b_out = jnp.sum(grad_hidden, axis=(0, 1))
    grad_w_out = jnp.einsum(
        "pte,ptd->ed", attended, grad_branch, preferred_element_type=jnp.float32
    )
    grad_attended = jnp.einsum(
        "ptd,ed->pte", grad_branch, out_all, preferred_element_type=jnp.float32
    )
    grad_attended = grad_attended.astype(jnp.bfloat16)
    scores = scores_of(queries, keys_all, key_mask)
    probs_full = jnp.exp(scores - logsum)
    grad_heads = grad_attended.reshape(pack_count, row_count, head_count, HD)
    grad_probs = jnp.einsum(
        "pqhe,pkhe->phqk", grad_heads, values_all, preferred_element_type=jnp.float32
    )
    row_delta = jnp.sum(grad_probs * probs_full, axis=-1, keepdims=True)
    grad_scores = (probs_full * (grad_probs - row_delta)).astype(jnp.bfloat16)
    probs_low = probs_full.astype(jnp.bfloat16)
    grad_queries = SCORE_SCALE * jnp.einsum(
        "phqk,pkhe->pqhe", grad_scores, keys_all, preferred_element_type=jnp.float32
    )
    grad_queries = grad_queries.reshape(pack_count, row_count, local_width).astype(jnp.bfloat16)
    key_count = lax.axis_size("context") * row_count
    grad_key_part = SCORE_SCALE * jnp.einsum(
        "phqk,pqhe->kphe", grad_scores, queries, preferred_element_type=jnp.float32
    )
    grad_value_part = jnp.einsum(
        "phqk,pqhe->kphe", probs_low, grad_heads, preferred_element_type=jnp.float32
    )
    summed = lax.psum_scatter(
        jnp.stack(
            (
                grad_key_part.reshape(key_count, pack_count, local_width),
                grad_value_part.reshape(key_count, pack_count, local_width),
            ),
            axis=2,
        ),
        "context",
        scatter_dimension=0,
        tiled=True,
    )
    grad_keys = summed[:, :, 0].astype(jnp.bfloat16)
    grad_values = summed[:, :, 1].astype(jnp.bfloat16)
    grad_normed1 = (
        jnp.einsum("pte,de->ptd", grad_queries, qkv_all[:, 0], preferred_element_type=jnp.float32)
        + jnp.einsum("tpe,de->ptd", grad_keys, qkv_all[:, 1], preferred_element_type=jnp.float32)
        + jnp.einsum("tpe,de->ptd", grad_values, qkv_all[:, 2], preferred_element_type=jnp.float32)
    )
    grad_normed1 = lax.psum(grad_normed1.astype(jnp.bfloat16), "tensor").astype(jnp.float32)
    grad_w_query = jnp.einsum(
        "ptd,pte->de", normed1, grad_queries, preferred_element_type=jnp.float32
    )
    grad_w_key = jnp.einsum("ptd,tpe->de", normed1, grad_keys, preferred_element_type=jnp.float32)
    grad_w_value = jnp.einsum(
        "ptd,tpe->de", normed1, grad_values, preferred_element_type=jnp.float32
    )
    grad_w_qkv = jnp.stack((grad_w_query, grad_w_key, grad_w_value), axis=1)
    grad_b_qv = jnp.stack(
        (
            jnp.sum(grad_queries.astype(jnp.float32), axis=(0, 1)),
            jnp.sum(grad_values.astype(jnp.float32), axis=(0, 1)),
        )
    ).reshape(2, head_count, HD)
    unused_one, first_pull = jax.vjp(layer_norm, base_rows, gain_one, shift_one)
    grad_base_norm, grad_gain_one, grad_shift_one = first_pull(grad_normed1)
    grad_tokens = grad_hidden + grad_base_norm
    shards = (
        lax.psum_scatter(
            grad_w_qkv.astype(jnp.bfloat16), "fsdp", scatter_dimension=0, tiled=True
        ).astype(jnp.float32),
        lax.psum_scatter(
            grad_b_qv.astype(jnp.bfloat16), "fsdp", scatter_dimension=2, tiled=True
        ).astype(jnp.float32),
        lax.psum_scatter(
            grad_w_out.astype(jnp.bfloat16), "fsdp", scatter_dimension=1, tiled=True
        ).astype(jnp.float32),
        lax.psum_scatter(
            grad_b_out.astype(jnp.bfloat16), "fsdp", scatter_dimension=0, tiled=True
        ).astype(jnp.float32),
        lax.psum_scatter(
            grad_w_fc.astype(jnp.bfloat16), "fsdp", scatter_dimension=0, tiled=True
        ).astype(jnp.float32),
        lax.psum_scatter(
            grad_b_fc.astype(jnp.bfloat16), "fsdp", scatter_dimension=1, tiled=True
        ).astype(jnp.float32),
        lax.psum_scatter(
            grad_w_proj.astype(jnp.bfloat16), "fsdp", scatter_dimension=1, tiled=True
        ).astype(jnp.float32),
        lax.psum_scatter(
            grad_b_proj.astype(jnp.bfloat16), "fsdp", scatter_dimension=0, tiled=True
        ).astype(jnp.float32),
        lax.psum_scatter(
            grad_gain_one.astype(jnp.bfloat16), "fsdp", scatter_dimension=0, tiled=True
        ).astype(jnp.float32),
        lax.psum_scatter(
            grad_shift_one.astype(jnp.bfloat16), "fsdp", scatter_dimension=0, tiled=True
        ).astype(jnp.float32),
        lax.psum_scatter(
            grad_gain_two.astype(jnp.bfloat16), "fsdp", scatter_dimension=0, tiled=True
        ).astype(jnp.float32),
        lax.psum_scatter(
            grad_shift_two.astype(jnp.bfloat16), "fsdp", scatter_dimension=0, tiled=True
        ).astype(jnp.float32),
    )
    reduced = (
        lax.psum(shards[0].astype(jnp.bfloat16), "context").astype(jnp.float32),
        lax.psum(shards[1].astype(jnp.bfloat16), "context").astype(jnp.float32),
        lax.psum(shards[2].astype(jnp.bfloat16), "context").astype(jnp.float32),
        lax.psum(shards[3].astype(jnp.bfloat16), "context").astype(jnp.float32),
        lax.psum(shards[4].astype(jnp.bfloat16), "context").astype(jnp.float32),
        lax.psum(shards[5].astype(jnp.bfloat16), "context").astype(jnp.float32),
        lax.psum(shards[6].astype(jnp.bfloat16), "context").astype(jnp.float32),
        lax.psum(shards[7].astype(jnp.bfloat16), "context").astype(jnp.float32),
        lax.psum(shards[8].astype(jnp.bfloat16), "context").astype(jnp.float32),
        lax.psum(shards[9].astype(jnp.bfloat16), "context").astype(jnp.float32),
        lax.psum(shards[10].astype(jnp.bfloat16), "context").astype(jnp.float32),
        lax.psum(shards[11].astype(jnp.bfloat16), "context").astype(jnp.float32),
    )
    return (
        mixed,
        grad_tokens,
        reduced[0],
        reduced[1],
        reduced[2],
        reduced[3],
        reduced[4],
        reduced[5],
        reduced[6],
        reduced[7],
        reduced[8],
        reduced[9],
        reduced[10],
        reduced[11],
    )


def swap(values, axis, distance):
    size = lax.axis_size(axis)
    return lax.ppermute(values, axis, [(i, i ^ distance) for i in range(size)])


def after(values, earlier):
    return lax.optimization_barrier((values, earlier))[0]


def sum_four(part):
    half = part.shape[-1] // 2
    low = lax.axis_index("tensor") % 2 == 0
    left, right = part[:, :half], part[:, half:]
    keep = jnp.where(low, left, right)
    got = swap(jnp.where(low, right, left), "tensor", 1)
    pair = (keep.astype(jnp.float32) + got.astype(jnp.float32)).astype(jnp.bfloat16)
    far = swap(pair, "tensor", 2)
    mine = (pair.astype(jnp.float32) + far.astype(jnp.float32)).astype(jnp.bfloat16)
    other = swap(mine, "tensor", 1)
    return jnp.concatenate(
        (jnp.where(low, mine, other), jnp.where(low, other, mine)), axis=-1
    ).astype(jnp.float32)


def dot_to(left, right, dims):
    return lax.dot_general(left, right, (dims, ((), ())), preferred_element_type=jnp.float32)


def norm_parts(values):
    mean = jnp.mean(values, axis=-1, keepdims=True)
    centred = values - mean
    spread = jnp.mean(centred * centred, axis=-1, keepdims=True)
    rate = lax.rsqrt(spread + EPSILON)
    return centred * rate, rate


def norm_back(grad, nhat, rate, gain):
    scaled = grad * gain
    inner = (
        scaled
        - jnp.mean(scaled, axis=-1, keepdims=True)
        - nhat * jnp.mean(scaled * nhat, axis=-1, keepdims=True)
    )
    return rate * inner, jnp.sum(grad * nhat, axis=0), jnp.sum(grad, axis=0)


def fast_body(
    tokens,
    segments,
    cotangent,
    w_qkv,
    b_qv,
    w_out,
    b_out,
    w_fc,
    b_fc,
    w_proj,
    b_proj,
    ln1_gain,
    ln1_shift,
    ln2_gain,
    ln2_shift,
):
    f32, bf16 = jnp.float32, jnp.bfloat16
    rows, width = tokens.shape[1:]
    half = width // 2
    heads = b_qv.shape[1]
    local = heads * HD
    first = lax.axis_index("fsdp") == 0

    def turn(values):
        other = jnp.concatenate((values[:, half:], values[:, :half]), axis=1)
        return jnp.where(first, values, other)

    def in_order(mine, theirs, axis):
        return jnp.where(
            first,
            jnp.concatenate((mine, theirs), axis=axis),
            jnp.concatenate((theirs, mine), axis=axis),
        )

    vectors = (ln1_gain, ln1_shift, ln2_gain, ln2_shift, b_out, b_proj)
    packed = jnp.concatenate(vectors + (b_qv.reshape(-1), b_fc.reshape(-1)))
    packed_far = swap(packed, "fsdp", 1)
    flat_qkv = w_qkv.reshape(half, 3 * local)
    qkv_far = swap(flat_qkv, "fsdp", 1)
    out_far = swap(after(w_out, qkv_far), "fsdp", 1)
    fc_far = swap(after(w_fc, out_far), "fsdp", 1)
    proj_far = swap(after(w_proj, fc_far), "fsdp", 1)

    def whole(index):
        far = packed_far[index * half : (index + 1) * half]
        return jnp.concatenate((vectors[index], far)).astype(f32)

    gain_one, shift_one, gain_two, shift_two, bias_out, bias_proj = [whole(i) for i in range(6)]
    at = 6 * half
    bias_qv = in_order(b_qv, packed_far[at : at + b_qv.size].reshape(b_qv.shape), 2)
    bias_qv = bias_qv.astype(f32).reshape(2, local)
    at += b_qv.size
    bias_fc = in_order(b_fc, packed_far[at:].reshape(b_fc.shape), 1).astype(f32).reshape(-1)

    base = turn(tokens[0]).astype(f32)
    cot = turn(cotangent[0])
    nhat_one, rate_one = norm_parts(base)
    normed1 = (nhat_one * gain_one + shift_one).astype(bf16)
    qkv_all = jnp.concatenate((flat_qkv, qkv_far), axis=0)
    bias_row = jnp.concatenate((bias_qv[0], jnp.zeros((local,), f32), bias_qv[1]))
    projected = (dot_to(normed1, qkv_all, ((1,), (0,))) + bias_row).astype(bf16)

    send = jnp.transpose(projected.reshape(rows, 3, heads, HD), (2, 0, 1, 3))
    send = send.reshape(heads, rows, 3 * HD)
    seg_cols = jnp.broadcast_to(segments[0].astype(bf16)[None, :, None], (heads, rows, HD))
    send = jnp.concatenate((send, seg_cols), axis=2)
    got = lax.all_to_all(send, "context", 0, 0, tiled=True).reshape(heads * rows, 4 * HD)
    queries, keys, values = got[:, :HD], got[:, HD : 2 * HD], got[:, 2 * HD : 3 * HD]
    seg_all = got[:, 3 * HD]
    position = jnp.arange(heads * rows, dtype=jnp.int32)
    seen = (seg_all[:, None] == seg_all[None, :]) & (position[None, :] <= position[:, None])
    scores = jnp.where(
        seen, SCORE_SCALE * dot_to(queries, keys, ((1,), (1,))), -MASK_FILL
    )
    row_top = jnp.max(scores, axis=-1, keepdims=True)
    exponent = jnp.exp(scores - row_top)
    row_total = jnp.sum(exponent, axis=-1, keepdims=True)
    pfull = exponent / row_total
    probs = pfull.astype(bf16)
    att_head = dot_to(probs, values, ((1,), (0,))).astype(bf16)
    att = lax.all_to_all(att_head.reshape(heads, rows, HD), "context", 0, 0, tiled=True)
    attended = jnp.transpose(att, (1, 0, 2)).reshape(rows, local)

    out_all = jnp.concatenate((w_out, out_far), axis=1)
    attn_part = dot_to(attended, out_all, ((1,), (0,))).astype(bf16)
    hidden = base + sum_four(attn_part) + bias_out
    nhat_two, rate_two = norm_parts(hidden)
    normed2 = (nhat_two * gain_two + shift_two).astype(bf16)
    fc_all = jnp.concatenate((w_fc, fc_far), axis=0)
    proj_all = jnp.concatenate((w_proj, proj_far), axis=1)
    pre_act = dot_to(normed2, fc_all, ((1,), (0,))) + bias_fc
    activ, gelu_pull = jax.vjp(gelu_tanh, pre_act)
    activ = activ.astype(bf16)
    grad_activ = dot_to(cot, proj_all, ((1,), (1,)))
    grad_pre = gelu_pull(grad_activ)[0].astype(bf16)
    grad_n2 = sum_four(dot_to(grad_pre, fc_all, ((1,), (1,))).astype(bf16))
    mlp_part = dot_to(activ, proj_all, ((1,), (0,))).astype(bf16)
    mixed = turn((hidden + sum_four(mlp_part) + bias_proj).astype(bf16))

    def reduced(mine, theirs, earlier):
        total = mine + swap(theirs.astype(bf16), "fsdp", 1).astype(f32)
        total = total.astype(bf16)
        if earlier is not None:
            total = after(total, earlier)
        return lax.psum(total, "context")

    grad_proj = dot_to(activ, cot, ((0,), (0,)))
    proj_sum = reduced(grad_proj[:, :half], grad_proj[:, half:], None)
    grad_fc = dot_to(normed2, grad_pre, ((0,), (0,)))
    fc_sum = reduced(grad_fc[:half], grad_fc[half:], proj_sum)

    grad_out = cot.astype(f32)
    back_two, grad_gain_two, grad_shift_two = norm_back(grad_n2, nhat_two, rate_two, gain_two)
    grad_hidden = grad_out + back_two
    grad_branch = grad_hidden.astype(bf16)
    grad_att = dot_to(grad_branch, out_all, ((1,), (1,))).astype(bf16)
    grad_att = jnp.transpose(grad_att.reshape(rows, heads, HD), (1, 0, 2))
    grad_head = lax.all_to_all(grad_att, "context", 0, 0, tiled=True).reshape(heads * rows, HD)
    grad_w_out = dot_to(attended, grad_branch, ((0,), (0,)))
    out_sum = reduced(grad_w_out[:, :half], grad_w_out[:, half:], fc_sum)

    grad_probs = dot_to(grad_head, values, ((1,), (1,)))
    row_delta = jnp.sum(grad_probs * pfull, axis=-1, keepdims=True)
    grad_scores = (pfull * (grad_probs - row_delta)).astype(bf16)
    grad_q = SCORE_SCALE * dot_to(grad_scores, keys, ((1,), (0,)))
    grad_k = SCORE_SCALE * dot_to(grad_scores, queries, ((0,), (0,)))
    grad_v = dot_to(probs, grad_head, ((0,), (0,)))
    back = jnp.concatenate((grad_q, grad_k, grad_v), axis=1).astype(bf16)
    back = lax.all_to_all(back.reshape(heads, rows, 3 * HD), "context", 0, 0, tiled=True)
    back = jnp.transpose(back.reshape(heads, rows, 3, HD), (1, 2, 0, 3)).reshape(rows, 3 * local)
    grad_n1 = sum_four(dot_to(back, qkv_all, ((1,), (1,))).astype(bf16))
    grad_qkv = dot_to(normed1, back, ((0,), (0,)))
    qkv_sum = reduced(grad_qkv[:half], grad_qkv[half:], out_sum)
    back_one, grad_gain_one, grad_shift_one = norm_back(grad_n1, nhat_one, rate_one, gain_one)
    grad_tokens = turn(grad_hidden + back_one)

    grad_b_qkv = jnp.sum(back.astype(f32), axis=0).reshape(3, heads, HD)
    grad_b_qv = jnp.stack((grad_b_qkv[0], grad_b_qkv[2]))
    grad_b_fc = jnp.sum(grad_pre.astype(f32), axis=0).reshape(b_fc.shape[0], -1)
    sums = (
        jnp.sum(grad_out, axis=0),
        jnp.sum(grad_hidden, axis=0),
        grad_gain_one,
        grad_shift_one,
        grad_gain_two,
        grad_shift_two,
    )

    def split(values, axis):
        left, right = jnp.split(values, 2, axis=axis)
        return jnp.where(first, left, right), jnp.where(first, right, left)

    qv_mine, qv_far = split(grad_b_qv, 2)
    fc_mine, fc_theirs = split(grad_b_fc, 1)
    near = jnp.concatenate([v[:half] for v in sums] + [qv_mine.reshape(-1), fc_mine.reshape(-1)])
    away = jnp.concatenate([v[half:] for v in sums] + [qv_far.reshape(-1), fc_theirs.reshape(-1)])
    small = near + swap(away, "fsdp", 1)
    small = small + swap(small, "context", 1)
    small = small + swap(small, "context", 2)
    pieces = [small[i * half : (i + 1) * half] for i in range(6)]
    at = 6 * half
    return (
        mixed[None],
        grad_tokens[None],
        qkv_sum.astype(f32).reshape(half, 3, local),
        small[at : at + b_qv.size].reshape(b_qv.shape),
        out_sum.astype(f32),
        pieces[1],
        fc_sum.astype(f32),
        small[at + b_qv.size :].reshape(b_fc.shape),
        proj_sum.astype(f32),
        pieces[0],
        pieces[2],
        pieces[3],
        pieces[4],
        pieces[5],
    )


def solution(mesh):
    sizes = mesh.shape
    even = sizes["fsdp"] == 2 and sizes["tensor"] == 4 and sizes["context"] == 4
    return jax.shard_map(
        fast_body if even else body,
        mesh=mesh,
        in_specs=(
            P("fsdp", "context", None),
            P("fsdp", "context"),
            P("fsdp", "context", None),
            P("fsdp", None, "tensor"),
            P(None, "tensor", "fsdp"),
            P("tensor", "fsdp"),
            P("fsdp"),
            P("fsdp", "tensor"),
            P("tensor", "fsdp"),
            P("tensor", "fsdp"),
            P("fsdp"),
            P("fsdp"),
            P("fsdp"),
            P("fsdp"),
            P("fsdp"),
        ),
        out_specs=(
            P("fsdp", "context", None),
            P("fsdp", "context", None),
            P("fsdp", None, "tensor"),
            P(None, "tensor", "fsdp"),
            P("tensor", "fsdp"),
            P("fsdp"),
            P("fsdp", "tensor"),
            P("tensor", "fsdp"),
            P("tensor", "fsdp"),
            P("fsdp"),
            P("fsdp"),
            P("fsdp"),
            P("fsdp"),
            P("fsdp"),
        ),
        check_vma=False,
    )
```

```python
import jax
import jax.numpy as jnp
from jax import lax
from jax.sharding import PartitionSpec as P

HD = 64


EPSILON = 1e-05
MASK_FILL = 1e30
SCORE_SCALE = 0.125


def layer_norm(values, gain, shift):
    mean = jnp.mean(values, axis=-1, keepdims=True)
    centred = values - mean
    spread = jnp.mean(centred * centred, axis=-1, keepdims=True)
    return centred * lax.rsqrt(spread + EPSILON) * gain + shift


def gelu_tanh(values):
    inner = 0.7978845608028654 * (values + 0.044715 * values * values * values)
    return 0.5 * values * (1.0 + jnp.tanh(inner))


def visible(segments, key_segments, first_row):
    row_count = segments.shape[1]
    query_pos = first_row + jnp.arange(row_count, dtype=jnp.int32)
    key_pos = jnp.arange(key_segments.shape[1], dtype=jnp.int32)
    same = segments.astype(jnp.float32)[:, :, None] == key_segments.astype(jnp.float32)[:, None, :]
    return same & (key_pos[None, None, :] <= query_pos[None, :, None])


def scores_of(queries, keys_all, key_mask):
    raw_scores = jnp.einsum(
        "pqhe,pkhe->phqk", queries, keys_all, preferred_element_type=jnp.float32
    )
    return jnp.where(key_mask[:, None], SCORE_SCALE * raw_scores, -MASK_FILL)


def body(
    tokens,
    segments,
    cotangent,
    w_qkv,
    b_qv,
    w_out,
    b_out,
    w_fc,
    b_fc,
    w_proj,
    b_proj,
    ln1_gain,
    ln1_shift,
    ln2_gain,
    ln2_shift,
):
    pack_count, row_count, model_width = tokens.shape
    head_count = b_qv.shape[1]
    local_width = head_count * HD
    gathered = (
        lax.all_gather(w_qkv, "fsdp", axis=0, tiled=True),
        lax.all_gather(w_out, "fsdp", axis=1, tiled=True),
        lax.all_gather(w_fc, "fsdp", axis=0, tiled=True),
        lax.all_gather(w_proj, "fsdp", axis=1, tiled=True),
        lax.all_gather(b_qv, "fsdp", axis=2, tiled=True),
        lax.all_gather(b_out, "fsdp", axis=0, tiled=True),
        lax.all_gather(b_fc, "fsdp", axis=1, tiled=True),
        lax.all_gather(b_proj, "fsdp", axis=0, tiled=True),
        lax.all_gather(ln1_gain, "fsdp", axis=0, tiled=True),
        lax.all_gather(ln1_shift, "fsdp", axis=0, tiled=True),
        lax.all_gather(ln2_gain, "fsdp", axis=0, tiled=True),
        lax.all_gather(ln2_shift, "fsdp", axis=0, tiled=True),
    )
    qkv_all = gathered[0]
    out_all = gathered[1]
    fc_all = gathered[2]
    proj_all = gathered[3]
    bias_qv = gathered[4].astype(jnp.float32).reshape(2, local_width)
    bias_out = gathered[5].astype(jnp.float32)
    bias_fc = gathered[6].astype(jnp.float32).reshape(-1)
    bias_proj = gathered[7].astype(jnp.float32)
    gain_one = gathered[8].astype(jnp.float32)
    shift_one = gathered[9].astype(jnp.float32)
    gain_two = gathered[10].astype(jnp.float32)
    shift_two = gathered[11].astype(jnp.float32)
    first_row = lax.axis_index("context") * row_count
    base_rows = tokens.astype(jnp.float32)
    normed1 = layer_norm(base_rows, gain_one, shift_one).astype(jnp.bfloat16)
    projected = jnp.einsum("ptd,dje->ptje", normed1, qkv_all, preferred_element_type=jnp.float32)
    queries_low = (projected[:, :, 0] + bias_qv[0]).astype(jnp.bfloat16)
    keys_low = projected[:, :, 1].astype(jnp.bfloat16)
    values_low = (projected[:, :, 2] + bias_qv[1]).astype(jnp.bfloat16)
    seg_low = segments.astype(jnp.bfloat16)
    fetched = (
        lax.all_gather(keys_low, "context", axis=1, tiled=True),
        lax.all_gather(values_low, "context", axis=1, tiled=True),
        lax.all_gather(seg_low, "context", axis=1, tiled=True),
    )
    keys_all = fetched[0].reshape(pack_count, -1, head_count, HD)
    values_all = fetched[1].reshape(pack_count, -1, head_count, HD)
    key_mask = visible(segments, fetched[2], first_row)
    queries = queries_low.reshape(pack_count, row_count, head_count, HD)
    scores = scores_of(queries, keys_all, key_mask)
    row_top = jnp.max(scores, axis=-1, keepdims=True)
    exponent = jnp.exp(scores - row_top)
    row_total = jnp.sum(exponent, axis=-1, keepdims=True)
    probs = (exponent / row_total).astype(jnp.bfloat16)
    logsum = row_top + jnp.log(row_total)
    attended = jnp.einsum("phqk,pkhe->pqhe", probs, values_all, preferred_element_type=jnp.float32)
    attended = attended.reshape(pack_count, row_count, local_width).astype(jnp.bfloat16)
    attn_part = jnp.einsum("pte,ed->ptd", attended, out_all, preferred_element_type=jnp.float32)
    hidden_state = base_rows + lax.psum(attn_part, "tensor") + bias_out
    normed2 = layer_norm(hidden_state, gain_two, shift_two).astype(jnp.bfloat16)
    pre_act = (
        jnp.einsum("ptd,df->ptf", normed2, fc_all, preferred_element_type=jnp.float32) + bias_fc
    )
    activ = gelu_tanh(pre_act).astype(jnp.bfloat16)
    mlp_part = jnp.einsum("ptf,fd->ptd", activ, proj_all, preferred_element_type=jnp.float32)
    mixed = (
        hidden_state
        + lax.psum(mlp_part.astype(jnp.bfloat16), "tensor").astype(jnp.float32)
        + bias_proj
    ).astype(jnp.bfloat16)
    grad_out = cotangent.astype(jnp.float32)
    grad_b_proj = jnp.sum(grad_out, axis=(0, 1))
    grad_w_proj = jnp.einsum("ptf,ptd->fd", activ, cotangent, preferred_element_type=jnp.float32)
    grad_activ = jnp.einsum("ptd,fd->ptf", cotangent, proj_all, preferred_element_type=jnp.float32)
    unused, gelu_pull = jax.vjp(gelu_tanh, pre_act)
    grad_pre = gelu_pull(grad_activ)[0].astype(jnp.bfloat16)
    grad_b_fc = jnp.sum(grad_pre.astype(jnp.float32), axis=(0, 1)).reshape(gathered[6].shape)
    grad_w_fc = jnp.einsum("ptd,ptf->df", normed2, grad_pre, preferred_element_type=jnp.float32)
    grad_normed2 = jnp.einsum("ptf,df->ptd", grad_pre, fc_all, preferred_element_type=jnp.float32)
    grad_normed2 = lax.psum(grad_normed2, "tensor")
    unused_two, norm_pull = jax.vjp(layer_norm, hidden_state, gain_two, shift_two)
    grad_hidden_norm, grad_gain_two, grad_shift_two = norm_pull(grad_normed2)
    grad_hidden = grad_out + grad_hidden_norm
    grad_branch = grad_hidden.astype(jnp.bfloat16)
    grad_b_out = jnp.sum(grad_hidden, axis=(0, 1))
    grad_w_out = jnp.einsum(
        "pte,ptd->ed", attended, grad_branch, preferred_element_type=jnp.float32
    )
    grad_attended = jnp.einsum(
        "ptd,ed->pte", grad_branch, out_all, preferred_element_type=jnp.float32
    )
    grad_attended = grad_attended.astype(jnp.bfloat16)
    scores = scores_of(queries, keys_all, key_mask)
    probs_full = jnp.exp(scores - logsum)
    grad_heads = grad_attended.reshape(pack_count, row_count, head_count, HD)
    grad_probs = jnp.einsum(
        "pqhe,pkhe->phqk", grad_heads, values_all, preferred_element_type=jnp.float32
    )
    row_delta = jnp.sum(grad_probs * probs_full, axis=-1, keepdims=True)
    grad_scores = (probs_full * (grad_probs - row_delta)).astype(jnp.bfloat16)
    probs_low = probs_full.astype(jnp.bfloat16)
    grad_queries = SCORE_SCALE * jnp.einsum(
        "phqk,pkhe->pqhe", grad_scores, keys_all, preferred_element_type=jnp.float32
    )
    grad_queries = grad_queries.reshape(pack_count, row_count, local_width).astype(jnp.bfloat16)
    key_count = lax.axis_size("context") * row_count
    grad_key_part = SCORE_SCALE * jnp.einsum(
        "phqk,pqhe->kphe", grad_scores, queries, preferred_element_type=jnp.float32
    )
    grad_value_part = jnp.einsum(
        "phqk,pqhe->kphe", probs_low, grad_heads, preferred_element_type=jnp.float32
    )
    summed = lax.psum_scatter(
        jnp.stack(
            (
                grad_key_part.reshape(key_count, pack_count, local_width),
                grad_value_part.reshape(key_count, pack_count, local_width),
            ),
            axis=2,
        ),
        "context",
        scatter_dimension=0,
        tiled=True,
    )
    grad_keys = summed[:, :, 0].astype(jnp.bfloat16)
    grad_values = summed[:, :, 1].astype(jnp.bfloat16)
    grad_normed1 = (
        jnp.einsum("pte,de->ptd", grad_queries, qkv_all[:, 0], preferred_element_type=jnp.float32)
        + jnp.einsum("tpe,de->ptd", grad_keys, qkv_all[:, 1], preferred_element_type=jnp.float32)
        + jnp.einsum("tpe,de->ptd", grad_values, qkv_all[:, 2], preferred_element_type=jnp.float32)
    )
    grad_normed1 = lax.psum(grad_normed1.astype(jnp.bfloat16), "tensor").astype(jnp.float32)
    grad_w_query = jnp.einsum(
        "ptd,pte->de", normed1, grad_queries, preferred_element_type=jnp.float32
    )
    grad_w_key = jnp.einsum("ptd,tpe->de", normed1, grad_keys, preferred_element_type=jnp.float32)
    grad_w_value = jnp.einsum(
        "ptd,tpe->de", normed1, grad_values, preferred_element_type=jnp.float32
    )
    grad_w_qkv = jnp.stack((grad_w_query, grad_w_key, grad_w_value), axis=1)
    grad_b_qv = jnp.stack(
        (
            jnp.sum(grad_queries.astype(jnp.float32), axis=(0, 1)),
            jnp.sum(grad_values.astype(jnp.float32), axis=(0, 1)),
        )
    ).reshape(2, head_count, HD)
    unused_one, first_pull = jax.vjp(layer_norm, base_rows, gain_one, shift_one)
    grad_base_norm, grad_gain_one, grad_shift_one = first_pull(grad_normed1)
    grad_tokens = grad_hidden + grad_base_norm
    shards = (
        lax.psum_scatter(
            grad_w_qkv.astype(jnp.bfloat16), "fsdp", scatter_dimension=0, tiled=True
        ).astype(jnp.float32),
        lax.psum_scatter(
            grad_b_qv.astype(jnp.bfloat16), "fsdp", scatter_dimension=2, tiled=True
        ).astype(jnp.float32),
        lax.psum_scatter(
            grad_w_out.astype(jnp.bfloat16), "fsdp", scatter_dimension=1, tiled=True
        ).astype(jnp.float32),
        lax.psum_scatter(
            grad_b_out.astype(jnp.bfloat16), "fsdp", scatter_dimension=0, tiled=True
        ).astype(jnp.float32),
        lax.psum_scatter(
            grad_w_fc.astype(jnp.bfloat16), "fsdp", scatter_dimension=0, tiled=True
        ).astype(jnp.float32),
        lax.psum_scatter(
            grad_b_fc.astype(jnp.bfloat16), "fsdp", scatter_dimension=1, tiled=True
        ).astype(jnp.float32),
        lax.psum_scatter(
            grad_w_proj.astype(jnp.bfloat16), "fsdp", scatter_dimension=1, tiled=True
        ).astype(jnp.float32),
        lax.psum_scatter(
            grad_b_proj.astype(jnp.bfloat16), "fsdp", scatter_dimension=0, tiled=True
        ).astype(jnp.float32),
        lax.psum_scatter(
            grad_gain_one.astype(jnp.bfloat16), "fsdp", scatter_dimension=0, tiled=True
        ).astype(jnp.float32),
        lax.psum_scatter(
            grad_shift_one.astype(jnp.bfloat16), "fsdp", scatter_dimension=0, tiled=True
        ).astype(jnp.float32),
        lax.psum_scatter(
            grad_gain_two.astype(jnp.bfloat16), "fsdp", scatter_dimension=0, tiled=True
        ).astype(jnp.float32),
        lax.psum_scatter(
            grad_shift_two.astype(jnp.bfloat16), "fsdp", scatter_dimension=0, tiled=True
        ).astype(jnp.float32),
    )
    reduced = (
        lax.psum(shards[0].astype(jnp.bfloat16), "context").astype(jnp.float32),
        lax.psum(shards[1].astype(jnp.bfloat16), "context").astype(jnp.float32),
        lax.psum(shards[2].astype(jnp.bfloat16), "context").astype(jnp.float32),
        lax.psum(shards[3].astype(jnp.bfloat16), "context").astype(jnp.float32),
        lax.psum(shards[4].astype(jnp.bfloat16), "context").astype(jnp.float32),
        lax.psum(shards[5].astype(jnp.bfloat16), "context").astype(jnp.float32),
        lax.psum(shards[6].astype(jnp.bfloat16), "context").astype(jnp.float32),
        lax.psum(shards[7].astype(jnp.bfloat16), "context").astype(jnp.float32),
        lax.psum(shards[8].astype(jnp.bfloat16), "context").astype(jnp.float32),
        lax.psum(shards[9].astype(jnp.bfloat16), "context").astype(jnp.float32),
        lax.psum(shards[10].astype(jnp.bfloat16), "context").astype(jnp.float32),
        lax.psum(shards[11].astype(jnp.bfloat16), "context").astype(jnp.float32),
    )
    return (
        mixed,
        grad_tokens,
        reduced[0],
        reduced[1],
        reduced[2],
        reduced[3],
        reduced[4],
        reduced[5],
        reduced[6],
        reduced[7],
        reduced[8],
        reduced[9],
        reduced[10],
        reduced[11],
    )


def swap(values, axis, distance):
    size = lax.axis_size(axis)
    return lax.ppermute(values, axis, [(i, i ^ distance) for i in range(size)])


def after(values, earlier):
    return lax.optimization_barrier((values, earlier))[0]


def sum_four(part):
    half = part.shape[-1] // 2
    low = lax.axis_index("tensor") % 2 == 0
    left, right = part[:, :half], part[:, half:]
    keep = jnp.where(low, left, right)
    got = swap(jnp.where(low, right, left), "tensor", 1)
    pair = (keep.astype(jnp.float32) + got.astype(jnp.float32)).astype(jnp.bfloat16)
    far = swap(pair, "tensor", 2)
    mine = (pair.astype(jnp.float32) + far.astype(jnp.float32)).astype(jnp.bfloat16)
    other = swap(mine, "tensor", 1)
    return jnp.concatenate(
        (jnp.where(low, mine, other), jnp.where(low, other, mine)), axis=-1
    ).astype(jnp.float32)


def dot_to(left, right, dims):
    return lax.dot_general(left, right, (dims, ((), ())), preferred_element_type=jnp.float32)


def norm_parts(values):
    mean = jnp.mean(values, axis=-1, keepdims=True)
    centred = values - mean
    spread = jnp.mean(centred * centred, axis=-1, keepdims=True)
    rate = lax.rsqrt(spread + EPSILON)
    return centred * rate, rate


def norm_back(grad, nhat, rate, gain):
    scaled = grad * gain
    inner = (
        scaled
        - jnp.mean(scaled, axis=-1, keepdims=True)
        - nhat * jnp.mean(scaled * nhat, axis=-1, keepdims=True)
    )
    return rate * inner, jnp.sum(grad * nhat, axis=0), jnp.sum(grad, axis=0)


def fast_body(
    tokens,
    segments,
    cotangent,
    w_qkv,
    b_qv,
    w_out,
    b_out,
    w_fc,
    b_fc,
    w_proj,
    b_proj,
    ln1_gain,
    ln1_shift,
    ln2_gain,
    ln2_shift,
):
    f32, bf16 = jnp.float32, jnp.bfloat16
    rows, width = tokens.shape[1:]
    half = width // 2
    heads = b_qv.shape[1]
    local = heads * HD
    first = lax.axis_index("fsdp") == 0

    def turn(values):
        other = jnp.concatenate((values[:, half:], values[:, :half]), axis=1)
        return jnp.where(first, values, other)

    def in_order(mine, theirs, axis):
        return jnp.where(
            first,
            jnp.concatenate((mine, theirs), axis=axis),
            jnp.concatenate((theirs, mine), axis=axis),
        )

    vectors = (ln1_gain, ln1_shift, ln2_gain, ln2_shift, b_out, b_proj)
    packed = jnp.concatenate(vectors + (b_qv.reshape(-1), b_fc.reshape(-1)))
    packed_far = swap(packed, "fsdp", 1)
    flat_qkv = w_qkv.reshape(half, 3 * local)
    qkv_far = swap(flat_qkv, "fsdp", 1)
    out_far = swap(after(w_out, qkv_far), "fsdp", 1)
    fc_far = swap(after(w_fc, qkv_far), "fsdp", 1)

    def whole(index):
        far = packed_far[index * half : (index + 1) * half]
        return jnp.concatenate((vectors[index], far)).astype(f32)

    gain_one, shift_one, gain_two, shift_two, bias_out, bias_proj = [whole(i) for i in range(6)]
    at = 6 * half
    bias_qv = in_order(b_qv, packed_far[at : at + b_qv.size].reshape(b_qv.shape), 2)
    bias_qv = bias_qv.astype(f32).reshape(2, local)
    at += b_qv.size
    bias_fc = in_order(b_fc, packed_far[at:].reshape(b_fc.shape), 1).astype(f32).reshape(-1)

    base = turn(tokens[0]).astype(f32)
    cot = turn(cotangent[0])
    nhat_one, rate_one = norm_parts(base)
    normed1 = (nhat_one * gain_one + shift_one).astype(bf16)
    qkv_all = jnp.concatenate((flat_qkv, qkv_far), axis=0)
    bias_row = jnp.concatenate((bias_qv[0], jnp.zeros((local,), f32), bias_qv[1]))
    projected = (dot_to(normed1, qkv_all, ((1,), (0,))) + bias_row).astype(bf16)

    send = jnp.transpose(projected.reshape(rows, 3, heads, HD), (2, 0, 1, 3))
    send = send.reshape(heads, rows, 3 * HD)
    seg_cols = jnp.broadcast_to(segments[0].astype(bf16)[None, :, None], (heads, rows, HD))
    send = jnp.concatenate((send, seg_cols), axis=2)
    got = lax.all_to_all(send, "context", 0, 0, tiled=True).reshape(heads * rows, 4 * HD)
    proj_far = swap(after(w_proj, got), "fsdp", 1)
    queries, keys, values = got[:, :HD], got[:, HD : 2 * HD], got[:, 2 * HD : 3 * HD]
    seg_all = got[:, 3 * HD]
    position = jnp.arange(heads * rows, dtype=jnp.int32)
    seen = (seg_all[:, None] == seg_all[None, :]) & (position[None, :] <= position[:, None])
    scores = jnp.where(
        seen, SCORE_SCALE * dot_to(queries, keys, ((1,), (1,))), -MASK_FILL
    )
    row_top = jnp.max(scores, axis=-1, keepdims=True)
    exponent = jnp.exp(scores - row_top)
    row_total = jnp.sum(exponent, axis=-1, keepdims=True)
    pfull = exponent / row_total
    probs = pfull.astype(bf16)
    att_head = dot_to(probs, values, ((1,), (0,))).astype(bf16)
    att_head, fc_far = lax.optimization_barrier((att_head, fc_far))
    att = lax.all_to_all(att_head.reshape(heads, rows, HD), "context", 0, 0, tiled=True)
    att, proj_far = lax.optimization_barrier((att, proj_far))
    attended = jnp.transpose(att, (1, 0, 2)).reshape(rows, local)

    out_all = jnp.concatenate((w_out, out_far), axis=1)
    attn_part = dot_to(attended, out_all, ((1,), (0,))).astype(bf16)
    hidden = base + sum_four(attn_part) + bias_out
    nhat_two, rate_two = norm_parts(hidden)
    normed2 = (nhat_two * gain_two + shift_two).astype(bf16)
    fc_all = jnp.concatenate((w_fc, fc_far), axis=0)
    proj_all = jnp.concatenate((w_proj, proj_far), axis=1)
    pre_act = dot_to(normed2, fc_all, ((1,), (0,))) + bias_fc
    activ, gelu_pull = jax.vjp(gelu_tanh, pre_act)
    activ = activ.astype(bf16)
    grad_activ = dot_to(cot, proj_all, ((1,), (1,)))
    grad_pre = gelu_pull(grad_activ)[0].astype(bf16)
    grad_proj = dot_to(activ, cot, ((0,), (0,)))
    proj_send = grad_proj[:, half:].astype(bf16)
    grad_pre, proj_send = lax.optimization_barrier((grad_pre, proj_send))
    grad_n2 = sum_four(dot_to(grad_pre, fc_all, ((1,), (1,))).astype(bf16))
    mlp_part = dot_to(activ, proj_all, ((1,), (0,))).astype(bf16)
    mixed = turn((hidden + sum_four(mlp_part) + bias_proj).astype(bf16))

    def own_half(mine, theirs):
        return (mine + swap(theirs.astype(bf16), "fsdp", 1).astype(f32)).astype(bf16)

    proj_total = own_half(grad_proj[:, :half], proj_send)
    grad_fc = dot_to(normed2, grad_pre, ((0,), (0,)))
    fc_total = own_half(grad_fc[:half], grad_fc[half:])

    grad_out = cot.astype(f32)
    back_two, grad_gain_two, grad_shift_two = norm_back(grad_n2, nhat_two, rate_two, gain_two)
    grad_hidden = grad_out + back_two
    grad_branch = grad_hidden.astype(bf16)
    grad_att = dot_to(grad_branch, out_all, ((1,), (1,))).astype(bf16)
    grad_att = jnp.transpose(grad_att.reshape(rows, heads, HD), (1, 0, 2))
    grad_head = lax.all_to_all(grad_att, "context", 0, 0, tiled=True).reshape(heads * rows, HD)
    grad_w_out = dot_to(attended, grad_branch, ((0,), (0,)))
    out_total = own_half(grad_w_out[:, :half], grad_w_out[:, half:])
    grad_head, proj_total = lax.optimization_barrier((grad_head, proj_total))
    proj_sum = lax.psum(proj_total, "context")

    grad_probs = dot_to(grad_head, values, ((1,), (1,)))
    row_delta = jnp.sum(grad_probs * pfull, axis=-1, keepdims=True)
    grad_scores = (pfull * (grad_probs - row_delta)).astype(bf16)
    grad_q = SCORE_SCALE * dot_to(grad_scores, keys, ((1,), (0,)))
    grad_k = SCORE_SCALE * dot_to(grad_scores, queries, ((0,), (0,)))
    grad_v = dot_to(probs, grad_head, ((0,), (0,)))
    back = jnp.concatenate((grad_q, grad_k, grad_v), axis=1).astype(bf16)
    back, fc_total, out_total = lax.optimization_barrier((back, fc_total, out_total))
    back = lax.all_to_all(back.reshape(heads, rows, 3 * HD), "context", 0, 0, tiled=True)
    back = jnp.transpose(back.reshape(heads, rows, 3, HD), (1, 2, 0, 3)).reshape(rows, 3 * local)
    grad_qkv = dot_to(normed1, back, ((0,), (0,)))
    qkv_send = grad_qkv[half:].astype(bf16)
    back, qkv_send = lax.optimization_barrier((back, qkv_send))
    qkv_total = own_half(grad_qkv[:half], qkv_send)
    grad_n1 = sum_four(dot_to(back, qkv_all, ((1,), (1,))).astype(bf16))
    last = lax.optimization_barrier((qkv_total, out_total, fc_total, proj_sum))
    qkv_sum, out_sum, fc_sum = lax.psum(last[:3], "context")
    proj_sum = last[3]
    back_one, grad_gain_one, grad_shift_one = norm_back(grad_n1, nhat_one, rate_one, gain_one)
    grad_tokens = turn(grad_hidden + back_one)

    grad_b_qkv = jnp.sum(back.astype(f32), axis=0).reshape(3, heads, HD)
    grad_b_qv = jnp.stack((grad_b_qkv[0], grad_b_qkv[2]))
    grad_b_fc = jnp.sum(grad_pre.astype(f32), axis=0).reshape(b_fc.shape[0], -1)
    sums = (
        jnp.sum(grad_out, axis=0),
        jnp.sum(grad_hidden, axis=0),
        grad_gain_one,
        grad_shift_one,
        grad_gain_two,
        grad_shift_two,
    )

    def split(values, axis):
        left, right = jnp.split(values, 2, axis=axis)
        return jnp.where(first, left, right), jnp.where(first, right, left)

    qv_mine, qv_far = split(grad_b_qv, 2)
    fc_mine, fc_theirs = split(grad_b_fc, 1)
    near = jnp.concatenate([v[:half] for v in sums] + [qv_mine.reshape(-1), fc_mine.reshape(-1)])
    away = jnp.concatenate([v[half:] for v in sums] + [qv_far.reshape(-1), fc_theirs.reshape(-1)])
    small = near + swap(away, "fsdp", 1)
    small = small + swap(small, "context", 1)
    small = small + swap(small, "context", 2)
    pieces = [small[i * half : (i + 1) * half] for i in range(6)]
    at = 6 * half
    return (
        mixed[None],
        grad_tokens[None],
        qkv_sum.astype(f32).reshape(half, 3, local),
        small[at : at + b_qv.size].reshape(b_qv.shape),
        out_sum.astype(f32),
        pieces[1],
        fc_sum.astype(f32),
        small[at + b_qv.size :].reshape(b_fc.shape),
        proj_sum.astype(f32),
        pieces[0],
        pieces[2],
        pieces[3],
        pieces[4],
        pieces[5],
    )


def solution(mesh):
    sizes = mesh.shape
    even = sizes["fsdp"] == 2 and sizes["tensor"] == 4 and sizes["context"] == 4
    return jax.shard_map(
        fast_body if even else body,
        mesh=mesh,
        in_specs=(
            P("fsdp", "context", None),
            P("fsdp", "context"),
            P("fsdp", "context", None),
            P("fsdp", None, "tensor"),
            P(None, "tensor", "fsdp"),
            P("tensor", "fsdp"),
            P("fsdp"),
            P("fsdp", "tensor"),
            P("tensor", "fsdp"),
            P("tensor", "fsdp"),
            P("fsdp"),
            P("fsdp"),
            P("fsdp"),
            P("fsdp"),
            P("fsdp"),
        ),
        out_specs=(
            P("fsdp", "context", None),
            P("fsdp", "context", None),
            P("fsdp", None, "tensor"),
            P(None, "tensor", "fsdp"),
            P("tensor", "fsdp"),
            P("fsdp"),
            P("fsdp", "tensor"),
            P("tensor", "fsdp"),
            P("tensor", "fsdp"),
            P("fsdp"),
            P("fsdp"),
            P("fsdp"),
            P("fsdp"),
            P("fsdp"),
        ),
        check_vma=False,
    )
```

```python
import jax
import jax.numpy as jnp
from jax import lax
from jax.sharding import PartitionSpec as P

HD = 64


EPSILON = 1e-05
MASK_FILL = 1e30
SCORE_SCALE = 0.125


def layer_norm(values, gain, shift):
    mean = jnp.mean(values, axis=-1, keepdims=True)
    centred = values - mean
    spread = jnp.mean(centred * centred, axis=-1, keepdims=True)
    return centred * lax.rsqrt(spread + EPSILON) * gain + shift


def gelu_tanh(values):
    inner = 0.7978845608028654 * (values + 0.044715 * values * values * values)
    return 0.5 * values * (1.0 + jnp.tanh(inner))


def visible(segments, key_segments, first_row):
    row_count = segments.shape[1]
    query_pos = first_row + jnp.arange(row_count, dtype=jnp.int32)
    key_pos = jnp.arange(key_segments.shape[1], dtype=jnp.int32)
    same = segments.astype(jnp.float32)[:, :, None] == key_segments.astype(jnp.float32)[:, None, :]
    return same & (key_pos[None, None, :] <= query_pos[None, :, None])


def scores_of(queries, keys_all, key_mask):
    raw_scores = jnp.einsum(
        "pqhe,pkhe->phqk", queries, keys_all, preferred_element_type=jnp.float32
    )
    return jnp.where(key_mask[:, None], SCORE_SCALE * raw_scores, -MASK_FILL)


def body(
    tokens,
    segments,
    cotangent,
    w_qkv,
    b_qv,
    w_out,
    b_out,
    w_fc,
    b_fc,
    w_proj,
    b_proj,
    ln1_gain,
    ln1_shift,
    ln2_gain,
    ln2_shift,
):
    pack_count, row_count, model_width = tokens.shape
    head_count = b_qv.shape[1]
    local_width = head_count * HD
    gathered = (
        lax.all_gather(w_qkv, "fsdp", axis=0, tiled=True),
        lax.all_gather(w_out, "fsdp", axis=1, tiled=True),
        lax.all_gather(w_fc, "fsdp", axis=0, tiled=True),
        lax.all_gather(w_proj, "fsdp", axis=1, tiled=True),
        lax.all_gather(b_qv, "fsdp", axis=2, tiled=True),
        lax.all_gather(b_out, "fsdp", axis=0, tiled=True),
        lax.all_gather(b_fc, "fsdp", axis=1, tiled=True),
        lax.all_gather(b_proj, "fsdp", axis=0, tiled=True),
        lax.all_gather(ln1_gain, "fsdp", axis=0, tiled=True),
        lax.all_gather(ln1_shift, "fsdp", axis=0, tiled=True),
        lax.all_gather(ln2_gain, "fsdp", axis=0, tiled=True),
        lax.all_gather(ln2_shift, "fsdp", axis=0, tiled=True),
    )
    qkv_all = gathered[0]
    out_all = gathered[1]
    fc_all = gathered[2]
    proj_all = gathered[3]
    bias_qv = gathered[4].astype(jnp.float32).reshape(2, local_width)
    bias_out = gathered[5].astype(jnp.float32)
    bias_fc = gathered[6].astype(jnp.float32).reshape(-1)
    bias_proj = gathered[7].astype(jnp.float32)
    gain_one = gathered[8].astype(jnp.float32)
    shift_one = gathered[9].astype(jnp.float32)
    gain_two = gathered[10].astype(jnp.float32)
    shift_two = gathered[11].astype(jnp.float32)
    first_row = lax.axis_index("context") * row_count
    base_rows = tokens.astype(jnp.float32)
    normed1 = layer_norm(base_rows, gain_one, shift_one).astype(jnp.bfloat16)
    projected = jnp.einsum("ptd,dje->ptje", normed1, qkv_all, preferred_element_type=jnp.float32)
    queries_low = (projected[:, :, 0] + bias_qv[0]).astype(jnp.bfloat16)
    keys_low = projected[:, :, 1].astype(jnp.bfloat16)
    values_low = (projected[:, :, 2] + bias_qv[1]).astype(jnp.bfloat16)
    seg_low = segments.astype(jnp.bfloat16)
    fetched = (
        lax.all_gather(keys_low, "context", axis=1, tiled=True),
        lax.all_gather(values_low, "context", axis=1, tiled=True),
        lax.all_gather(seg_low, "context", axis=1, tiled=True),
    )
    keys_all = fetched[0].reshape(pack_count, -1, head_count, HD)
    values_all = fetched[1].reshape(pack_count, -1, head_count, HD)
    key_mask = visible(segments, fetched[2], first_row)
    queries = queries_low.reshape(pack_count, row_count, head_count, HD)
    scores = scores_of(queries, keys_all, key_mask)
    row_top = jnp.max(scores, axis=-1, keepdims=True)
    exponent = jnp.exp(scores - row_top)
    row_total = jnp.sum(exponent, axis=-1, keepdims=True)
    probs = (exponent / row_total).astype(jnp.bfloat16)
    logsum = row_top + jnp.log(row_total)
    attended = jnp.einsum("phqk,pkhe->pqhe", probs, values_all, preferred_element_type=jnp.float32)
    attended = attended.reshape(pack_count, row_count, local_width).astype(jnp.bfloat16)
    attn_part = jnp.einsum("pte,ed->ptd", attended, out_all, preferred_element_type=jnp.float32)
    hidden_state = base_rows + lax.psum(attn_part, "tensor") + bias_out
    normed2 = layer_norm(hidden_state, gain_two, shift_two).astype(jnp.bfloat16)
    pre_act = (
        jnp.einsum("ptd,df->ptf", normed2, fc_all, preferred_element_type=jnp.float32) + bias_fc
    )
    activ = gelu_tanh(pre_act).astype(jnp.bfloat16)
    mlp_part = jnp.einsum("ptf,fd->ptd", activ, proj_all, preferred_element_type=jnp.float32)
    mixed = (
        hidden_state
        + lax.psum(mlp_part.astype(jnp.bfloat16), "tensor").astype(jnp.float32)
        + bias_proj
    ).astype(jnp.bfloat16)
    grad_out = cotangent.astype(jnp.float32)
    grad_b_proj = jnp.sum(grad_out, axis=(0, 1))
    grad_w_proj = jnp.einsum("ptf,ptd->fd", activ, cotangent, preferred_element_type=jnp.float32)
    grad_activ = jnp.einsum("ptd,fd->ptf", cotangent, proj_all, preferred_element_type=jnp.float32)
    unused, gelu_pull = jax.vjp(gelu_tanh, pre_act)
    grad_pre = gelu_pull(grad_activ)[0].astype(jnp.bfloat16)
    grad_b_fc = jnp.sum(grad_pre.astype(jnp.float32), axis=(0, 1)).reshape(gathered[6].shape)
    grad_w_fc = jnp.einsum("ptd,ptf->df", normed2, grad_pre, preferred_element_type=jnp.float32)
    grad_normed2 = jnp.einsum("ptf,df->ptd", grad_pre, fc_all, preferred_element_type=jnp.float32)
    grad_normed2 = lax.psum(grad_normed2, "tensor")
    unused_two, norm_pull = jax.vjp(layer_norm, hidden_state, gain_two, shift_two)
    grad_hidden_norm, grad_gain_two, grad_shift_two = norm_pull(grad_normed2)
    grad_hidden = grad_out + grad_hidden_norm
    grad_branch = grad_hidden.astype(jnp.bfloat16)
    grad_b_out = jnp.sum(grad_hidden, axis=(0, 1))
    grad_w_out = jnp.einsum(
        "pte,ptd->ed", attended, grad_branch, preferred_element_type=jnp.float32
    )
    grad_attended = jnp.einsum(
        "ptd,ed->pte", grad_branch, out_all, preferred_element_type=jnp.float32
    )
    grad_attended = grad_attended.astype(jnp.bfloat16)
    scores = scores_of(queries, keys_all, key_mask)
    probs_full = jnp.exp(scores - logsum)
    grad_heads = grad_attended.reshape(pack_count, row_count, head_count, HD)
    grad_probs = jnp.einsum(
        "pqhe,pkhe->phqk", grad_heads, values_all, preferred_element_type=jnp.float32
    )
    row_delta = jnp.sum(grad_probs * probs_full, axis=-1, keepdims=True)
    grad_scores = (probs_full * (grad_probs - row_delta)).astype(jnp.bfloat16)
    probs_low = probs_full.astype(jnp.bfloat16)
    grad_queries = SCORE_SCALE * jnp.einsum(
        "phqk,pkhe->pqhe", grad_scores, keys_all, preferred_element_type=jnp.float32
    )
    grad_queries = grad_queries.reshape(pack_count, row_count, local_width).astype(jnp.bfloat16)
    key_count = lax.axis_size("context") * row_count
    grad_key_part = SCORE_SCALE * jnp.einsum(
        "phqk,pqhe->kphe", grad_scores, queries, preferred_element_type=jnp.float32
    )
    grad_value_part = jnp.einsum(
        "phqk,pqhe->kphe", probs_low, grad_heads, preferred_element_type=jnp.float32
    )
    summed = lax.psum_scatter(
        jnp.stack(
            (
                grad_key_part.reshape(key_count, pack_count, local_width),
                grad_value_part.reshape(key_count, pack_count, local_width),
            ),
            axis=2,
        ),
        "context",
        scatter_dimension=0,
        tiled=True,
    )
    grad_keys = summed[:, :, 0].astype(jnp.bfloat16)
    grad_values = summed[:, :, 1].astype(jnp.bfloat16)
    grad_normed1 = (
        jnp.einsum("pte,de->ptd", grad_queries, qkv_all[:, 0], preferred_element_type=jnp.float32)
        + jnp.einsum("tpe,de->ptd", grad_keys, qkv_all[:, 1], preferred_element_type=jnp.float32)
        + jnp.einsum("tpe,de->ptd", grad_values, qkv_all[:, 2], preferred_element_type=jnp.float32)
    )
    grad_normed1 = lax.psum(grad_normed1.astype(jnp.bfloat16), "tensor").astype(jnp.float32)
    grad_w_query = jnp.einsum(
        "ptd,pte->de", normed1, grad_queries, preferred_element_type=jnp.float32
    )
    grad_w_key = jnp.einsum("ptd,tpe->de", normed1, grad_keys, preferred_element_type=jnp.float32)
    grad_w_value = jnp.einsum(
        "ptd,tpe->de", normed1, grad_values, preferred_element_type=jnp.float32
    )
    grad_w_qkv = jnp.stack((grad_w_query, grad_w_key, grad_w_value), axis=1)
    grad_b_qv = jnp.stack(
        (
            jnp.sum(grad_queries.astype(jnp.float32), axis=(0, 1)),
            jnp.sum(grad_values.astype(jnp.float32), axis=(0, 1)),
        )
    ).reshape(2, head_count, HD)
    unused_one, first_pull = jax.vjp(layer_norm, base_rows, gain_one, shift_one)
    grad_base_norm, grad_gain_one, grad_shift_one = first_pull(grad_normed1)
    grad_tokens = grad_hidden + grad_base_norm
    shards = (
        lax.psum_scatter(
            grad_w_qkv.astype(jnp.bfloat16), "fsdp", scatter_dimension=0, tiled=True
        ).astype(jnp.float32),
        lax.psum_scatter(
            grad_b_qv.astype(jnp.bfloat16), "fsdp", scatter_dimension=2, tiled=True
        ).astype(jnp.float32),
        lax.psum_scatter(
            grad_w_out.astype(jnp.bfloat16), "fsdp", scatter_dimension=1, tiled=True
        ).astype(jnp.float32),
        lax.psum_scatter(
            grad_b_out.astype(jnp.bfloat16), "fsdp", scatter_dimension=0, tiled=True
        ).astype(jnp.float32),
        lax.psum_scatter(
            grad_w_fc.astype(jnp.bfloat16), "fsdp", scatter_dimension=0, tiled=True
        ).astype(jnp.float32),
        lax.psum_scatter(
            grad_b_fc.astype(jnp.bfloat16), "fsdp", scatter_dimension=1, tiled=True
        ).astype(jnp.float32),
        lax.psum_scatter(
            grad_w_proj.astype(jnp.bfloat16), "fsdp", scatter_dimension=1, tiled=True
        ).astype(jnp.float32),
        lax.psum_scatter(
            grad_b_proj.astype(jnp.bfloat16), "fsdp", scatter_dimension=0, tiled=True
        ).astype(jnp.float32),
        lax.psum_scatter(
            grad_gain_one.astype(jnp.bfloat16), "fsdp", scatter_dimension=0, tiled=True
        ).astype(jnp.float32),
        lax.psum_scatter(
            grad_shift_one.astype(jnp.bfloat16), "fsdp", scatter_dimension=0, tiled=True
        ).astype(jnp.float32),
        lax.psum_scatter(
            grad_gain_two.astype(jnp.bfloat16), "fsdp", scatter_dimension=0, tiled=True
        ).astype(jnp.float32),
        lax.psum_scatter(
            grad_shift_two.astype(jnp.bfloat16), "fsdp", scatter_dimension=0, tiled=True
        ).astype(jnp.float32),
    )
    reduced = (
        lax.psum(shards[0].astype(jnp.bfloat16), "context").astype(jnp.float32),
        lax.psum(shards[1].astype(jnp.bfloat16), "context").astype(jnp.float32),
        lax.psum(shards[2].astype(jnp.bfloat16), "context").astype(jnp.float32),
        lax.psum(shards[3].astype(jnp.bfloat16), "context").astype(jnp.float32),
        lax.psum(shards[4].astype(jnp.bfloat16), "context").astype(jnp.float32),
        lax.psum(shards[5].astype(jnp.bfloat16), "context").astype(jnp.float32),
        lax.psum(shards[6].astype(jnp.bfloat16), "context").astype(jnp.float32),
        lax.psum(shards[7].astype(jnp.bfloat16), "context").astype(jnp.float32),
        lax.psum(shards[8].astype(jnp.bfloat16), "context").astype(jnp.float32),
        lax.psum(shards[9].astype(jnp.bfloat16), "context").astype(jnp.float32),
        lax.psum(shards[10].astype(jnp.bfloat16), "context").astype(jnp.float32),
        lax.psum(shards[11].astype(jnp.bfloat16), "context").astype(jnp.float32),
    )
    return (
        mixed,
        grad_tokens,
        reduced[0],
        reduced[1],
        reduced[2],
        reduced[3],
        reduced[4],
        reduced[5],
        reduced[6],
        reduced[7],
        reduced[8],
        reduced[9],
        reduced[10],
        reduced[11],
    )


def swap(values, axis, distance):
    size = lax.axis_size(axis)
    return lax.ppermute(values, axis, [(i, i ^ distance) for i in range(size)])


def after(values, earlier):
    return lax.optimization_barrier((values, earlier))[0]


def sum_four(part):
    half = part.shape[-1] // 2
    low = lax.axis_index("tensor") % 2 == 0
    left, right = part[:, :half], part[:, half:]
    keep = jnp.where(low, left, right)
    got = swap(jnp.where(low, right, left), "tensor", 1)
    pair = (keep.astype(jnp.float32) + got.astype(jnp.float32)).astype(jnp.bfloat16)
    far = swap(pair, "tensor", 2)
    mine = (pair.astype(jnp.float32) + far.astype(jnp.float32)).astype(jnp.bfloat16)
    other = swap(mine, "tensor", 1)
    return jnp.concatenate(
        (jnp.where(low, mine, other), jnp.where(low, other, mine)), axis=-1
    ).astype(jnp.float32)


def dot_to(left, right, dims):
    return lax.dot_general(left, right, (dims, ((), ())), preferred_element_type=jnp.float32)


def norm_parts(values):
    mean = jnp.mean(values, axis=-1, keepdims=True)
    centred = values - mean
    spread = jnp.mean(centred * centred, axis=-1, keepdims=True)
    rate = lax.rsqrt(spread + EPSILON)
    return centred * rate, rate


def norm_back(grad, nhat, rate, gain):
    scaled = grad * gain
    inner = (
        scaled
        - jnp.mean(scaled, axis=-1, keepdims=True)
        - nhat * jnp.mean(scaled * nhat, axis=-1, keepdims=True)
    )
    return rate * inner, jnp.sum(grad * nhat, axis=0), jnp.sum(grad, axis=0)


def fast_body(
    tokens,
    segments,
    cotangent,
    w_qkv,
    b_qv,
    w_out,
    b_out,
    w_fc,
    b_fc,
    w_proj,
    b_proj,
    ln1_gain,
    ln1_shift,
    ln2_gain,
    ln2_shift,
):
    f32, bf16 = jnp.float32, jnp.bfloat16
    rows, width = tokens.shape[1:]
    half = width // 2
    heads = b_qv.shape[1]
    local = heads * HD
    first = lax.axis_index("fsdp") == 0

    def turn(values):
        other = jnp.concatenate((values[:, half:], values[:, :half]), axis=1)
        return jnp.where(first, values, other)

    def in_order(mine, theirs, axis):
        return jnp.where(
            first,
            jnp.concatenate((mine, theirs), axis=axis),
            jnp.concatenate((theirs, mine), axis=axis),
        )

    vectors = (ln1_gain, ln1_shift, ln2_gain, ln2_shift, b_out, b_proj)
    packed = jnp.concatenate(vectors + (b_qv.reshape(-1), b_fc.reshape(-1)))
    packed_far = swap(packed, "fsdp", 1)
    flat_qkv = w_qkv.reshape(half, 3 * local)
    qkv_far = swap(flat_qkv, "fsdp", 1)
    out_far = swap(after(w_out, qkv_far), "fsdp", 1)
    fc_far = swap(after(w_fc, qkv_far), "fsdp", 1)

    def whole(index):
        far = packed_far[index * half : (index + 1) * half]
        return jnp.concatenate((vectors[index], far)).astype(f32)

    gain_one, shift_one, gain_two, shift_two, bias_out, bias_proj = [whole(i) for i in range(6)]
    at = 6 * half
    bias_qv = in_order(b_qv, packed_far[at : at + b_qv.size].reshape(b_qv.shape), 2)
    bias_qv = bias_qv.astype(f32).reshape(2, local)
    at += b_qv.size
    bias_fc = in_order(b_fc, packed_far[at:].reshape(b_fc.shape), 1).astype(f32).reshape(-1)

    base = turn(tokens[0]).astype(f32)
    cot = turn(cotangent[0])
    nhat_one, rate_one = norm_parts(base)
    normed1 = (nhat_one * gain_one + shift_one).astype(bf16)
    qkv_all = jnp.concatenate((flat_qkv, qkv_far), axis=0)
    bias_row = jnp.concatenate((bias_qv[0], jnp.zeros((local,), f32), bias_qv[1]))
    projected = (dot_to(normed1, qkv_all, ((1,), (0,))) + bias_row).astype(bf16)

    send = jnp.transpose(projected.reshape(rows, 3, heads, HD), (2, 0, 1, 3))
    send = send.reshape(heads, rows, 3 * HD)
    seg_cols = jnp.broadcast_to(segments[0].astype(bf16)[None, :, None], (heads, rows, HD))
    send = jnp.concatenate((send, seg_cols), axis=2)
    got = lax.all_to_all(send, "context", 0, 0, tiled=True).reshape(heads * rows, 4 * HD)
    proj_far = swap(after(w_proj, got), "fsdp", 1)
    queries, keys, values = got[:, :HD], got[:, HD : 2 * HD], got[:, 2 * HD : 3 * HD]
    seg_all = got[:, 3 * HD]
    position = jnp.arange(heads * rows, dtype=jnp.int32)
    seen = (seg_all[:, None] == seg_all[None, :]) & (position[None, :] <= position[:, None])
    scores = jnp.where(
        seen, SCORE_SCALE * dot_to(queries, keys, ((1,), (1,))), -MASK_FILL
    )
    row_top = jnp.max(scores, axis=-1, keepdims=True)
    exponent = jnp.exp(scores - row_top)
    row_total = jnp.sum(exponent, axis=-1, keepdims=True)
    pfull = exponent / row_total
    probs = pfull.astype(bf16)
    att_head = dot_to(probs, values, ((1,), (0,))).astype(bf16)
    att = lax.all_to_all(att_head.reshape(heads, rows, HD), "context", 0, 0, tiled=True)
    att, fc_far = lax.optimization_barrier((att, fc_far))
    attended = jnp.transpose(att, (1, 0, 2)).reshape(rows, local)

    out_all = jnp.concatenate((w_out, out_far), axis=1)
    attn_part = dot_to(attended, out_all, ((1,), (0,))).astype(bf16)
    attn_sum, proj_far = lax.optimization_barrier((sum_four(attn_part), proj_far))
    hidden = base + attn_sum + bias_out
    nhat_two, rate_two = norm_parts(hidden)
    normed2 = (nhat_two * gain_two + shift_two).astype(bf16)
    fc_all = jnp.concatenate((w_fc, fc_far), axis=0)
    pre_act = dot_to(normed2, fc_all, ((1,), (0,))) + bias_fc
    proj_all = jnp.concatenate((w_proj, proj_far), axis=1)
    activ, gelu_pull = jax.vjp(gelu_tanh, pre_act)
    activ = activ.astype(bf16)
    grad_activ = dot_to(cot, proj_all, ((1,), (1,)))
    grad_pre = gelu_pull(grad_activ)[0].astype(bf16)
    grad_proj = dot_to(activ, cot, ((0,), (0,)))
    proj_send = grad_proj[:, half:].astype(bf16)
    grad_pre, proj_send = lax.optimization_barrier((grad_pre, proj_send))
    grad_n2 = sum_four(dot_to(grad_pre, fc_all, ((1,), (1,))).astype(bf16))
    mlp_part = dot_to(activ, proj_all, ((1,), (0,))).astype(bf16)
    mixed = turn((hidden + sum_four(mlp_part) + bias_proj).astype(bf16))

    def own_half(mine, theirs):
        return (mine + swap(theirs.astype(bf16), "fsdp", 1).astype(f32)).astype(bf16)

    proj_total = own_half(grad_proj[:, :half], proj_send)
    grad_fc = dot_to(normed2, grad_pre, ((0,), (0,)))
    fc_total = own_half(grad_fc[:half], grad_fc[half:])

    grad_out = cot.astype(f32)
    back_two, grad_gain_two, grad_shift_two = norm_back(grad_n2, nhat_two, rate_two, gain_two)
    grad_hidden = grad_out + back_two
    grad_branch = grad_hidden.astype(bf16)
    grad_att = dot_to(grad_branch, out_all, ((1,), (1,))).astype(bf16)
    grad_att = jnp.transpose(grad_att.reshape(rows, heads, HD), (1, 0, 2))
    grad_head = lax.all_to_all(grad_att, "context", 0, 0, tiled=True).reshape(heads * rows, HD)
    grad_w_out = dot_to(attended, grad_branch, ((0,), (0,)))
    out_total = own_half(grad_w_out[:, :half], grad_w_out[:, half:])
    grad_head, proj_total = lax.optimization_barrier((grad_head, proj_total))
    proj_sum = lax.psum(proj_total, "context")

    grad_probs = dot_to(grad_head, values, ((1,), (1,)))
    row_delta = jnp.sum(grad_probs * pfull, axis=-1, keepdims=True)
    grad_scores = (pfull * (grad_probs - row_delta)).astype(bf16)
    grad_q = SCORE_SCALE * dot_to(grad_scores, keys, ((1,), (0,)))
    grad_k = SCORE_SCALE * dot_to(grad_scores, queries, ((0,), (0,)))
    grad_v = dot_to(probs, grad_head, ((0,), (0,)))
    back = jnp.concatenate((grad_q, grad_k, grad_v), axis=1).astype(bf16)
    back = lax.all_to_all(back.reshape(heads, rows, 3 * HD), "context", 0, 0, tiled=True)
    back = jnp.transpose(back.reshape(heads, rows, 3, HD), (1, 2, 0, 3)).reshape(rows, 3 * local)
    back, fc_total, out_total = lax.optimization_barrier((back, fc_total, out_total))
    grad_qkv = dot_to(normed1, back, ((0,), (0,)))
    qkv_send = grad_qkv[half:].astype(bf16)
    back, qkv_send = lax.optimization_barrier((back, qkv_send))
    qkv_total = own_half(grad_qkv[:half], qkv_send)
    grad_n1 = sum_four(dot_to(back, qkv_all, ((1,), (1,))).astype(bf16))
    last = lax.optimization_barrier((qkv_total, out_total, fc_total, proj_sum))
    qkv_sum, out_sum, fc_sum = lax.psum(last[:3], "context")
    proj_sum = last[3]
    back_one, grad_gain_one, grad_shift_one = norm_back(grad_n1, nhat_one, rate_one, gain_one)
    grad_tokens = turn(grad_hidden + back_one)

    grad_b_qkv = jnp.sum(back.astype(f32), axis=0).reshape(3, heads, HD)
    grad_b_qv = jnp.stack((grad_b_qkv[0], grad_b_qkv[2]))
    grad_b_fc = jnp.sum(grad_pre.astype(f32), axis=0).reshape(b_fc.shape[0], -1)
    sums = (
        jnp.sum(grad_out, axis=0),
        jnp.sum(grad_hidden, axis=0),
        grad_gain_one,
        grad_shift_one,
        grad_gain_two,
        grad_shift_two,
    )

    def split(values, axis):
        left, right = jnp.split(values, 2, axis=axis)
        return jnp.where(first, left, right), jnp.where(first, right, left)

    qv_mine, qv_far = split(grad_b_qv, 2)
    fc_mine, fc_theirs = split(grad_b_fc, 1)
    near = jnp.concatenate([v[:half] for v in sums] + [qv_mine.reshape(-1), fc_mine.reshape(-1)])
    away = jnp.concatenate([v[half:] for v in sums] + [qv_far.reshape(-1), fc_theirs.reshape(-1)])
    small = near + swap(away, "fsdp", 1)
    small = small + swap(small, "context", 1)
    small = small + swap(small, "context", 2)
    pieces = [small[i * half : (i + 1) * half] for i in range(6)]
    at = 6 * half
    return (
        mixed[None],
        grad_tokens[None],
        qkv_sum.astype(f32).reshape(half, 3, local),
        small[at : at + b_qv.size].reshape(b_qv.shape),
        out_sum.astype(f32),
        pieces[1],
        fc_sum.astype(f32),
        small[at + b_qv.size :].reshape(b_fc.shape),
        proj_sum.astype(f32),
        pieces[0],
        pieces[2],
        pieces[3],
        pieces[4],
        pieces[5],
    )


def solution(mesh):
    sizes = mesh.shape
    even = sizes["fsdp"] == 2 and sizes["tensor"] == 4 and sizes["context"] == 4
    return jax.shard_map(
        fast_body if even else body,
        mesh=mesh,
        in_specs=(
            P("fsdp", "context", None),
            P("fsdp", "context"),
            P("fsdp", "context", None),
            P("fsdp", None, "tensor"),
            P(None, "tensor", "fsdp"),
            P("tensor", "fsdp"),
            P("fsdp"),
            P("fsdp", "tensor"),
            P("tensor", "fsdp"),
            P("tensor", "fsdp"),
            P("fsdp"),
            P("fsdp"),
            P("fsdp"),
            P("fsdp"),
            P("fsdp"),
        ),
        out_specs=(
            P("fsdp", "context", None),
            P("fsdp", "context", None),
            P("fsdp", None, "tensor"),
            P(None, "tensor", "fsdp"),
            P("tensor", "fsdp"),
            P("fsdp"),
            P("fsdp", "tensor"),
            P("tensor", "fsdp"),
            P("tensor", "fsdp"),
            P("fsdp"),
            P("fsdp"),
            P("fsdp"),
            P("fsdp"),
            P("fsdp"),
        ),
        check_vma=False,
    )
```
